128 devices in a mesh: dp: 16 (over y, x_hi, core), tensor: 8 (over z, x_lo).
Axes of the slice: x: 4 (x_hi: 2, x_lo: 2; x = x_hi * 2 + x_lo), y: 4, z: 4, core: 2. Of those that a mesh axis runs over, the one named last changes fastest.
Arguments:
- tokens: bfloat16 [3072, 4096], P(('dp', 'tensor')), may hold values from -24 to 24
- w_gate: bfloat16 [4096, 14336], P('dp', 'tensor'), may hold values from -0.09375 to 0.09375
- w_up: bfloat16 [4096, 14336], P('dp', 'tensor'), may hold values from -0.09375 to 0.09375
- w_down: bfloat16 [14336, 4096], P('tensor', 'dp'), may hold values from -0.046875 to 0.046875
- cotangent: bfloat16 [3072, 4096], P(('dp', 'tensor')), may hold values from -24 to 24
Outputs:
- d_tokens: bfloat16 [3072, 4096], P(('dp', 'tensor'))
- d_w_gate: float32 [4096, 14336], P('dp', 'tensor')
- d_w_up: float32 [4096, 14336], P('dp', 'tensor')
- d_w_down: float32 [14336, 4096], P('tensor', 'dp')
The draws below stay inside these ranges and needn't reach their ends.
All inputs are finite; a program needn't handle non-finite values.
Results may differ from the reference program's by a relative error of at most 0.019.
Values may be sent and summed in bfloat16 or wider, within the bound.
No kernel may reach another device: no remote copies, remote signals or barrier semaphores. Data moves between devices by JAX's collectives and lax.ppermute only.
A program may use at most 192 MiB of HBM per device.

```python
import jax
import jax.numpy as jnp
from jax import lax

D = 4096
FF = 14336
GROUP_TOK = 192
TOKENS = 3072
N_DP = 16


def raised(result, key, source, target, parts, factor):
    owner, partner = [(jnp.arange(result.shape[dim]) // (result.shape[dim] // parts)).reshape([-1 if axis == dim else 1 for axis in range(result.ndim)]) for dim in (source, target)]
    chosen = jax.random.permutation(key, parts)[partner]
    strong = (owner == chosen) | (owner == (partner + parts // 2) % parts)
    return jnp.where(strong, factor * result, result)


def block_levels(own_key, dims, cuts, least, high):
    gain = 1.0
    for position, shards_of in cuts:
        heights = jax.random.uniform(jax.random.fold_in(jax.random.fold_in(own_key, 6), position), (shards_of,), jnp.float32, least / len(cuts), high / len(cuts))
        gain = gain * jnp.repeat(jnp.exp(heights), dims[position] // shards_of).reshape((-1,) + (1,) * (len(dims) - 1 - position))
    return gain


def scatter_about(rng, shape, deviation, limit, split=(), kind=jnp.bfloat16):
    entries = jax.random.normal(rng, shape, jnp.float32) * deviation
    if len(split) > 0:
        entries = block_levels(rng, shape, split, -0.22, 0.18) * entries
    return jnp.clip(entries, min=-limit, max=limit).astype(kind)


def bell_draw_with(rng, dims, spread, limit, split, heavy, held_as=jnp.bfloat16):
    values = spread * jax.random.normal(rng, dims, jnp.float32)
    if split:
        values = values * block_levels(rng, dims, split, -0.22, 0.18)
    return jnp.clip(raised(values, jax.random.fold_in(rng, 3), *heavy), -limit, limit).astype(held_as)


def setup_inputs(seed: int = 0) -> dict:
    splits = jax.random.split(jax.random.key(seed), 6)
    tokens = bell_draw_with(splits[0], (TOKENS, D), 1.0, 24.0, ((0, 128),), (0, 1, 128, 5.5))
    w_gate = scatter_about(splits[1], (D, FF), D ** -0.5, 0.09375, ((0, 16), (1, 8)))
    w_up = scatter_about(splits[2], (D, FF), D ** -0.5, 0.09375, ((0, 16), (1, 8)))
    w_down = scatter_about(splits[3], (FF, D), FF ** -0.5, 0.046875, ((0, 8), (1, 16)))
    cotangent = bell_draw_with(splits[4], (TOKENS, D), 1.0, 24.0, ((0, 128),), (0, 1, 128, 5.5))
    return dict(tokens=tokens, w_gate=w_gate, w_up=w_up, w_down=w_down, cotangent=cotangent)


def reference(tokens, w_gate, w_up, w_down, cotangent):
    gate = jnp.dot(tokens, w_gate, preferred_element_type=jnp.float32)
    up = jnp.dot(tokens, w_up, preferred_element_type=jnp.float32)
    sig = jax.nn.sigmoid(gate)
    swish = gate * sig
    hidden = (swish * up).astype(jnp.bfloat16)
    d_hidden = jnp.dot(cotangent, w_down.T, preferred_element_type=jnp.float32)
    d_up = (d_hidden * swish).astype(jnp.bfloat16)
    d_gate = (d_hidden * up * (sig + swish * (1.0 - sig))).astype(jnp.bfloat16)
    d_tokens = (jnp.dot(d_gate, w_gate.T, preferred_element_type=jnp.float32)
                + jnp.dot(d_up, w_up.T, preferred_element_type=jnp.float32)).astype(jnp.bfloat16)
    group_tokens = tokens.reshape(N_DP, GROUP_TOK, D)
    group_cot = cotangent.reshape(N_DP, GROUP_TOK, D)
    group_gate = d_gate.reshape(N_DP, GROUP_TOK, FF)
    group_up = d_up.reshape(N_DP, GROUP_TOK, FF)
    group_hidden = hidden.reshape(N_DP, GROUP_TOK, FF)

    def accumulate(carry, items):
        rows, cots, dg, du, hid = items
        part_gate = jnp.dot(rows.T, dg, preferred_element_type=jnp.float32).astype(jnp.bfloat16)
        part_up = jnp.dot(rows.T, du, preferred_element_type=jnp.float32).astype(jnp.bfloat16)
        part_down = jnp.dot(hid.T, cots, preferred_element_type=jnp.float32).astype(jnp.bfloat16)
        return (carry[0] + part_gate.astype(jnp.float32),
                carry[1] + part_up.astype(jnp.float32),
                carry[2] + part_down.astype(jnp.float32)), None

    start = (jnp.zeros((D, FF), jnp.float32), jnp.zeros((D, FF), jnp.float32), jnp.zeros((FF, D), jnp.float32))
    sums, unused = lax.scan(accumulate, start, (group_tokens, group_cot, group_gate, group_up, group_hidden))
    return d_tokens, sums[0], sums[1], sums[2]
```

```python
import jax
import jax.numpy as jnp
from jax import lax
from jax.sharding import PartitionSpec as P


def shift_y(x, k):
    return lax.ppermute(x, "dp", [(i, (i // 4 + k) % 4 * 4 + i % 4) for i in range(16)])


def shift_z(x, k):
    return lax.ppermute(x, "tensor", [(i, (i // 2 + k) % 4 * 2 + i % 2) for i in range(8)])


def swap_h(x):
    return lax.ppermute(x, "dp", [(i, i ^ 2) for i in range(16)])


def swap_c(x):
    return lax.ppermute(x, "dp", [(i, i ^ 1) for i in range(16)])


def swap_l(x):
    return lax.ppermute(x, "tensor", [(i, i ^ 1) for i in range(8)])


def gather_direct(x, shift):
    return jnp.concatenate([x, shift(x, -1), shift(x, -2), shift(x, -3)], 0)


def gather_ring(x, shift):
    half = x.shape[0] // 2
    after = shift(x, -1)
    before = shift(x, 1)
    low = shift(before[:half], 1)
    high = shift(after[half:], -1)
    return jnp.concatenate([x, after, low, high, before], 0)


def add(*terms):
    total = terms[0].astype(jnp.float32)
    for term in terms[1:]:
        total = total + term.astype(jnp.float32)
    return total.astype(jnp.bfloat16)


def scatter_direct(x, shift):
    n = x.shape[0] // 4
    parts = [x[n * k : n * (k + 1)] for k in range(4)]
    return add(parts[0], *[shift(parts[k], k) for k in (1, 2, 3)])


def scatter_ring(x, shift):
    n = x.shape[0] // 4
    half = n // 2
    own, after, far, before = [x[n * k : n * (k + 1)] for k in range(4)]
    low = shift(far[:half], 1)
    high = shift(far[half:], -1)
    after_high = shift(after[half:], 1)
    before_low = shift(before[:half], -1)
    after_low = shift(add(after[:half], low), 1)
    before_high = shift(add(before[half:], high), -1)
    return jnp.concatenate(
        [add(own[:half], after_low, before_low), add(own[half:], after_high, before_high)], 0
    )


def exchange_y(pieces, y):
    out = pieces
    for k in (1, 2, 3):
        sent = lax.dynamic_index_in_dim(pieces, (y + k) % 4, 0, keepdims=True)
        out = lax.dynamic_update_index_in_dim(out, shift_y(sent, k), (y - k) % 4, 0)
    return out


def shards(tokens, w_gate, w_up, w_down, cotangent):
    depth, local_ff = w_gate.shape
    rows, model = tokens.shape
    part_ff = local_ff // 4
    me = lax.axis_index("dp")
    y, h, c = me // 4, me // 2 % 2, me % 2

    def to_relative(x):
        x = x.reshape(rows, 4, 2, 2, depth)
        x = jnp.where(h == 1, x[:, :, ::-1], x)
        x = jnp.where(c == 1, x[:, :, :, ::-1], x)
        return x.transpose(0, 2, 3, 1, 4).reshape(rows, model)

    def from_relative(x):
        x = x.reshape(rows, 2, 2, 4, depth).transpose(0, 3, 1, 2, 4)
        x = jnp.where(h == 1, x[:, :, ::-1], x)
        x = jnp.where(c == 1, x[:, :, :, ::-1], x)
        return x.reshape(rows, model)

    def gather_rows(x):
        mine = to_relative(x)
        other = swap_l(mine)
        return jnp.concatenate(
            [
                gather_ring(gather_direct(mine, shift_y), shift_z),
                gather_ring(gather_direct(other, shift_z), shift_y),
            ],
            0,
        )

    def scatter_rows(x):
        n = x.shape[0] // 2
        mine = scatter_direct(scatter_ring(x[:n], shift_z), shift_y)
        other = scatter_direct(scatter_ring(x[n:], shift_y), shift_z)
        return from_relative(add(mine, swap_l(other)))

    def gather_blocks(x, axis):
        far = swap_h(x)
        return jnp.concatenate([x, swap_c(x), far, swap_c(far)], axis)

    def scatter_blocks(x, axis):
        near, near_c, far, far_c = jnp.split(x, 4, axis)
        far = swap_h(add(far, swap_c(far_c)))
        return add(near, swap_c(near_c), far)

    pair = jnp.concatenate(
        [w_gate.reshape(depth, 4, part_ff), w_up.reshape(depth, 4, part_ff)], 2
    ).transpose(1, 0, 2)
    pair = exchange_y(pair, y).reshape(4 * depth, 2 * part_ff)
    pair = gather_blocks(pair, 0)
    all_tokens = gather_rows(tokens)
    down = exchange_y(w_down.reshape(4, part_ff, depth), y)
    down = down.transpose(1, 0, 2).reshape(part_ff, 4 * depth)
    down = gather_blocks(down, 1)
    all_cot = gather_rows(cotangent)

    both = jnp.dot(all_tokens, pair, preferred_element_type=jnp.float32)
    gate = both[:, :part_ff]
    up = both[:, part_ff:]
    sig = jax.nn.sigmoid(gate)
    swish = gate * sig
    hidden = (swish * up).astype(jnp.bfloat16)
    down_grad = lax.dot_general(
        hidden, all_cot, (((0,), (0,)), ((), ())), preferred_element_type=jnp.float32
    ).astype(jnp.bfloat16)
    d_hidden = lax.dot_general(
        all_cot, down, (((1,), (1,)), ((), ())), preferred_element_type=jnp.float32
    )
    d_up = (d_hidden * swish).astype(jnp.bfloat16)
    d_gate = (d_hidden * up * (sig + swish * (1.0 - sig))).astype(jnp.bfloat16)
    pair_d = jnp.concatenate([d_gate, d_up], 1)
    pair_grad = lax.dot_general(
        all_tokens, pair_d, (((0,), (0,)), ((), ())), preferred_element_type=jnp.float32
    ).astype(jnp.bfloat16)
    partial = lax.dot_general(
        pair_d, pair, (((1,), (1,)), ((), ())), preferred_element_type=jnp.float32
    ).astype(jnp.bfloat16)

    d_tokens = scatter_rows(partial)
    down_grad = scatter_blocks(down_grad, 1).reshape(part_ff, 4, depth).transpose(1, 0, 2)
    d_w_down = exchange_y(down_grad, y).reshape(local_ff, depth).astype(jnp.float32)
    pair_grad = scatter_blocks(pair_grad, 0).reshape(4, depth, 2 * part_ff)
    pair_grad = exchange_y(pair_grad, y).transpose(1, 0, 2).astype(jnp.float32)
    d_w_gate = pair_grad[:, :, :part_ff].reshape(depth, local_ff)
    d_w_up = pair_grad[:, :, part_ff:].reshape(depth, local_ff)
    return (d_tokens, d_w_gate, d_w_up, d_w_down)


def solution(mesh):
    return jax.shard_map(
        shards,
        mesh=mesh,
        in_specs=(
            P(("dp", "tensor"), None),
            P("dp", "tensor"),
            P("dp", "tensor"),
            P("tensor", "dp"),
            P(("dp", "tensor"), None),
        ),
        out_specs=(
            P(("dp", "tensor"), None),
            P("dp", "tensor"),
            P("dp", "tensor"),
            P("tensor", "dp"),
        ),
        check_vma=False,
    )
```

```python
import jax
import jax.numpy as jnp
from jax import lax
from jax.sharding import PartitionSpec as P


def device_perm(target):
    pairs = []
    for i in range(128):
        y, h, c, z, l = i // 32, i // 16 % 2, i // 8 % 2, i // 2 % 4, i % 2
        y, h, c, z, l = target(y, h, c, z, l)
        pairs.append((i, (((y % 4 * 2 + h) * 2 + c) * 4 + z % 4) * 2 + l))
    return pairs


def send(x, target):
    return lax.ppermute(x, ("dp", "tensor"), device_perm(target))


def shift_y(x, k):
    return send(x, lambda y, h, c, z, l: (y + k, h, c, z, l))


def shift_first(x, k):
    return send(
        x, lambda y, h, c, z, l: (y, h, c, z + k, l) if c else (y + k, h, c, z, l)
    )


def shift_second(x, k):
    return send(
        x, lambda y, h, c, z, l: (y + k, h, c, z, l) if c else (y, h, c, z + k, l)
    )


def swap_h(x):
    return send(x, lambda y, h, c, z, l: (y, 1 - h, c, z, l))


def swap_c(x):
    return send(x, lambda y, h, c, z, l: (y, h, 1 - c, z, l))


def swap_l(x):
    return send(x, lambda y, h, c, z, l: (y, h, c, z, 1 - l))


def held(x, *until):
    return lax.optimization_barrier((x, until))[0]


def add(*terms):
    total = terms[0].astype(jnp.float32)
    for term in terms[1:]:
        total = total + term.astype(jnp.float32)
    return total.astype(jnp.bfloat16)


def send_pieces(pieces, y):
    out = pieces
    for k in (2, 1, 3):
        sent = lax.dynamic_index_in_dim(pieces, (y + k) % 4, 0, keepdims=True)
        out = lax.dynamic_update_index_in_dim(out, shift_y(sent, k), (y - k) % 4, 0)
    return out


def shards(tokens, w_gate, w_up, w_down, cotangent):
    depth, local_ff = w_gate.shape
    rows, model = tokens.shape
    part_ff = local_ff // 4
    me = lax.axis_index("dp")
    y, h, c = me // 4, me // 2 % 2, me % 2

    def to_relative(x):
        x = x.reshape(-1, 4, 2, 2, depth)
        x = jnp.where(h == 1, x[:, :, ::-1], x)
        x = jnp.where(c == 1, x[:, :, :, ::-1], x)
        return x.transpose(0, 3, 2, 1, 4).reshape(-1, model)

    def from_relative(x):
        x = x.reshape(-1, 2, 2, 4, depth).transpose(0, 3, 2, 1, 4)
        x = jnp.where(h == 1, x[:, :, ::-1], x)
        x = jnp.where(c == 1, x[:, :, :, ::-1], x)
        return x.reshape(-1, model)

    def columns(blocks):
        return jnp.concatenate([b[j] for b in blocks for j in range(4)], 1)

    both_rows = jnp.concatenate([tokens, cotangent], 0)
    both_l = swap_l(both_rows)
    pair = jnp.concatenate(
        [w_gate.T.reshape(4, part_ff, depth), w_up.T.reshape(4, part_ff, depth)], 1
    )
    pair = send_pieces(pair, y)
    base = to_relative(jnp.concatenate([both_rows, both_l], 0))
    far = shift_first(base, 2)
    after, before = shift_first(base, -1), shift_first(base, 1)
    pair_h = swap_h(pair)
    pair_c = swap_c(pair)

    def rows_of(start):
        pick = lambda x: [x[start : start + rows], x[start + 2 * rows : start + 3 * rows]]
        return jnp.concatenate([*pick(base), *pick(after), *pick(far), *pick(before)], 0)

    def second_near(x):
        return shift_second(x, -1), shift_second(x, 1)

    def second_far(after, before):
        half = after.shape[0] // 2
        return shift_second(before[:half], 1), shift_second(after[half:], -1)

    tok, cot = rows_of(0), rows_of(rows)
    tok_after, tok_before = second_near(tok)
    down = send_pieces(held(w_down.reshape(4, part_ff, depth), far, after, before), y)
    tok_low, tok_high = second_far(tok_after, tok_before)
    cot_after, cot_before = second_near(held(cot, tok_after, tok_before))
    down_h = swap_h(held(down, pair_h))
    cot_low, cot_high = second_far(cot_after, cot_before)
    pair_hc = swap_c(pair_h)
    down_c = swap_c(down)
    down_hc = swap_c(down_h)
    tok = jnp.concatenate([tok, tok_after, tok_low, tok_high, tok_before], 0)
    cot = jnp.concatenate([cot, cot_after, cot_low, cot_high, cot_before], 0)
    pair = columns([pair, pair_h, pair_c, pair_hc])
    down = columns([down, down_h, down_c, down_hc])

    def dot(a, b, dim_a, dim_b):
        return lax.dot_general(
            a, b, (((dim_a,), (dim_b,)), ((), ())), preferred_element_type=jnp.float32
        )

    gate_up = dot(pair, tok, 1, 1)
    gate = gate_up[:part_ff]
    up = gate_up[part_ff:]
    sig = jax.nn.sigmoid(gate)
    swish = gate * sig
    hidden = (swish * up).astype(jnp.bfloat16)
    d_hidden = dot(down, cot, 1, 1)
    d_up = (d_hidden * swish).astype(jnp.bfloat16)
    d_gate = (d_hidden * up * (sig + swish * (1.0 - sig))).astype(jnp.bfloat16)
    pair_d = jnp.concatenate([d_gate, d_up], 0)
    down_grad = dot(hidden, cot, 1, 0).astype(jnp.bfloat16)
    pair_grad = dot(pair_d, tok, 1, 0).astype(jnp.bfloat16)
    partial = dot(pair_d, pair, 0, 0).astype(jnp.bfloat16)

    half_model, quarter = model // 2, model // 4

    def sum_c(grad):
        return add(grad[:, :half_model], swap_c(grad[:, half_model:]))

    def sum_h(grad, far):
        return add(grad[:, :quarter], far)

    def sum_y(grad):
        n = grad.shape[0]
        pieces = grad.reshape(n, 4, depth).transpose(1, 0, 2)
        return send_pieces(pieces, y).reshape(4 * n, depth).astype(jnp.float32)

    down_grad = sum_c(down_grad)
    pair_grad = sum_c(pair_grad)
    down_far = swap_h(down_grad[:, quarter:])
    gate_far = swap_h(pair_grad[:part_ff, quarter:])
    up_far = swap_h(held(pair_grad[part_ff:, quarter:], down_far))

    n = partial.shape[0] // 4
    half = n // 2
    own, after, far, before = [partial[n * k : n * (k + 1)] for k in range(4)]
    low, high = shift_second(far[:half], 1), shift_second(far[half:], -1)
    after = jnp.concatenate([add(after[:half], low), after[half:]], 0)
    before = jnp.concatenate([before[:half], add(before[half:], high)], 0)
    own = add(own, shift_second(after, 1), shift_second(before, -1))
    n = n // 4
    parts = [own[n * k : n * (k + 1)] for k in range(4)]
    own = add(
        parts[0], shift_first(parts[2], 2), shift_first(parts[1], 1), shift_first(parts[3], -1)
    )
    d_tokens = from_relative(add(own[:rows], swap_l(own[rows:])))

    d_w_down = sum_y(sum_h(down_grad, down_far))
    d_w_gate = sum_y(sum_h(pair_grad[:part_ff], gate_far)).T
    d_w_up = sum_y(sum_h(pair_grad[part_ff:], up_far)).T
    return (d_tokens, d_w_gate, d_w_up, d_w_down)


def solution(mesh):
    return jax.shard_map(
        shards,
        mesh=mesh,
        in_specs=(
            P(("dp", "tensor"), None),
            P("dp", "tensor"),
            P("dp", "tensor"),
            P("tensor", "dp"),
            P(("dp", "tensor"), None),
        ),
        out_specs=(
            P(("dp", "tensor"), None),
            P("dp", "tensor"),
            P("dp", "tensor"),
            P("tensor", "dp"),
        ),
        check_vma=False,
    )
```

```python
import jax
import jax.numpy as jnp
from jax import lax
from jax.sharding import PartitionSpec as P


def device_perm(target):
    pairs = []
    for i in range(128):
        y, h, c, z, l = i // 32, i // 16 % 2, i // 8 % 2, i // 2 % 4, i % 2
        y, h, c, z, l = target(y, h, c, z, l)
        pairs.append((i, (((y % 4 * 2 + h) * 2 + c) * 4 + z % 4) * 2 + l))
    return pairs


def send(x, target):
    return lax.ppermute(x, ("dp", "tensor"), device_perm(target))


def shift_y(x, k):
    return send(x, lambda y, h, c, z, l: (y + k, h, c, z, l))


def shift_first(x, k):
    return send(
        x, lambda y, h, c, z, l: (y, h, c, z + k, l) if c else (y + k, h, c, z, l)
    )


def shift_second(x, k):
    return send(
        x, lambda y, h, c, z, l: (y + k, h, c, z, l) if c else (y, h, c, z + k, l)
    )


def swap_h(x):
    return send(x, lambda y, h, c, z, l: (y, 1 - h, c, z, l))


def swap_c(x):
    return send(x, lambda y, h, c, z, l: (y, h, 1 - c, z, l))


def swap_l(x):
    return send(x, lambda y, h, c, z, l: (y, h, c, z, 1 - l))


def sync(*arrays):
    return lax.optimization_barrier(arrays)


def add(*terms):
    total = terms[0].astype(jnp.float32)
    for term in terms[1:]:
        total = total + term.astype(jnp.float32)
    return total.astype(jnp.bfloat16)


def exchange_y(pieces):
    groups = [[4 * i + hc for i in range(4)] for hc in range(4)]
    return lax.all_to_all(pieces, "dp", 0, 0, axis_index_groups=groups, tiled=True)


def shards(tokens, w_gate, w_up, w_down, cotangent):
    depth, local_ff = w_gate.shape
    rows, model = tokens.shape
    part_ff = local_ff // 4
    me = lax.axis_index("dp")
    h, c = me // 2 % 2, me % 2

    def to_relative(x):
        x = x.reshape(-1, 4, 2, 2, depth)
        x = jnp.where(h == 1, x[:, :, ::-1], x)
        x = jnp.where(c == 1, x[:, :, :, ::-1], x)
        return x.transpose(0, 3, 2, 1, 4).reshape(-1, model)

    def from_relative(x):
        x = x.reshape(-1, 2, 2, 4, depth).transpose(0, 3, 2, 1, 4)
        x = jnp.where(h == 1, x[:, :, ::-1], x)
        x = jnp.where(c == 1, x[:, :, :, ::-1], x)
        return x.reshape(-1, model)

    def columns(blocks):
        return jnp.concatenate([b[j] for b in blocks for j in range(4)], 1)

    def dot(a, b, dim_a, dim_b):
        return lax.dot_general(
            a, b, (((dim_a,), (dim_b,)), ((), ())), preferred_element_type=jnp.float32
        )

    def second_near(x):
        return shift_second(x, -1), shift_second(x, 1)

    def second_far(after, before):
        half = after.shape[0] // 2
        return shift_second(before[:half], 1), shift_second(after[half:], -1)

    half_model, quarter = model // 2, model // 4

    both_rows = to_relative(jnp.concatenate([tokens, cotangent], 0))
    gate_w = w_gate.T.reshape(4, part_ff, depth)
    up_w = w_up.T.reshape(4, part_ff, depth)
    down_w = w_down.reshape(4, part_ff, depth)
    both_l, gate_w, up_w = sync(swap_l(both_rows), exchange_y(gate_w), up_w)

    base = jnp.concatenate(
        [both_rows[:rows], both_l[:rows], both_rows[rows:], both_l[rows:]], 0
    )
    gate_h, far, after, before, up_w = sync(
        swap_h(gate_w),
        shift_first(base, 2),
        shift_first(base, -1),
        shift_first(base, 1),
        exchange_y(up_w),
    )

    tok, cot = [
        jnp.concatenate([x[i : i + 2 * rows] for x in (base, after, far, before)], 0)
        for i in (0, 2 * rows)
    ]
    gate_w = columns([gate_w, gate_h])
    up_h, tok_near, down_w, gate_c, cot = sync(
        swap_h(up_w), second_near(tok), exchange_y(down_w), swap_c(gate_w), cot
    )

    up_w = columns([up_w, up_h])
    down_h, tok_far, cot_near, up_w = sync(
        swap_h(down_w), second_far(*tok_near), second_near(cot), up_w
    )

    tok = jnp.concatenate([tok, tok_near[0], *tok_far, tok_near[1]], 0)
    tok_n, tok_c = tok[:, :half_model], tok[:, half_model:]
    gate = dot(gate_w, tok_n, 1, 1) + dot(gate_c, tok_c, 1, 1)
    up = dot(up_w, tok_n, 1, 1)
    sig = jax.nn.sigmoid(gate)
    swish = gate * sig
    slope = sig + swish * (1.0 - sig)
    down_w = columns([down_w, down_h])
    down_c, up_c, cot_far, swish, slope, up = sync(
        swap_c(down_w), swap_c(up_w), second_far(*cot_near), swish, slope, up
    )

    def add_c(grad, got):
        return add(grad[:, :half_model], got)

    def pieces_of(grad):
        return grad.reshape(-1, 4, depth).transpose(1, 0, 2)

    def finish(pieces):
        return pieces.reshape(-1, depth).astype(jnp.float32)

    up = up + dot(up_c, tok_c, 1, 1)
    hidden = (swish * up).astype(jnp.bfloat16)
    cot = jnp.concatenate([cot, cot_near[0], *cot_far, cot_near[1]], 0)
    down_grad = dot(hidden, cot, 1, 0).astype(jnp.bfloat16)
    d_hidden = dot(down_w, cot[:, :half_model], 1, 1) + dot(down_c, cot[:, half_model:], 1, 1)
    d_up = (d_hidden * swish).astype(jnp.bfloat16)
    d_gate = (d_hidden * up * slope).astype(jnp.bfloat16)
    pair_d = jnp.concatenate([d_gate, d_up], 0)
    part_n = dot(pair_d, jnp.concatenate([gate_w, up_w], 0), 0, 0).astype(jnp.bfloat16)
    part_c = dot(pair_d, jnp.concatenate([gate_c, up_c], 0), 0, 0).astype(jnp.bfloat16)
    down_far, part_n, part_c, pair_d = sync(
        swap_c(down_grad[:, half_model:]), part_n, part_c, pair_d
    )

    n = part_n.shape[0] // 4
    own, after, far, before = [
        (part_n[n * k : n * (k + 1)], part_c[n * k : n * (k + 1)]) for k in range(4)
    ]
    down_grad = add_c(down_grad, down_far)
    pair_grad = dot(pair_d, tok, 1, 0).astype(jnp.bfloat16)
    down_far, low, high, pair_far = sync(
        swap_h(down_grad[:, quarter:]),
        shift_second(far[0], 1),
        shift_second(far[1], -1),
        swap_c(pair_grad[:, half_model:]),
    )

    pair_grad = add_c(pair_grad, pair_far)
    down_grad = pieces_of(add(down_grad[:, :quarter], down_far))
    after = jnp.concatenate([add(after[0], low), after[1]], 0)
    before = jnp.concatenate([before[0], add(before[1], high)], 0)
    gate_far, after, before, down_grad = sync(
        swap_h(pair_grad[:part_ff, quarter:]),
        shift_second(after, 1),
        shift_second(before, -1),
        exchange_y(down_grad),
    )

    gate_grad = pieces_of(add(pair_grad[:part_ff, :quarter], gate_far))
    own = add(jnp.concatenate(own, 0), after, before).reshape(2, 4, -1, half_model)
    own, after, far, before = [own[:, k].reshape(-1, half_model) for k in range(4)]
    up_far, far, after, before, gate_grad = sync(
        swap_h(pair_grad[part_ff:, quarter:]),
        shift_first(far, 2),
        shift_first(after, 1),
        shift_first(before, -1),
        exchange_y(gate_grad),
    )

    up_grad = pieces_of(add(pair_grad[part_ff:, :quarter], up_far))
    own = add(own, far, after, before).reshape(2, 2, rows, half_model)
    other = swap_l(own[:, 1].reshape(2 * rows, half_model)).reshape(2, rows, half_model)
    own = add(own[:, 0], other)
    d_tokens = from_relative(jnp.concatenate([own[0], own[1]], 1))
    d_w_down = finish(down_grad)
    d_w_gate = finish(gate_grad).T
    d_w_up = finish(exchange_y(up_grad)).T
    return (d_tokens, d_w_gate, d_w_up, d_w_down)


def solution(mesh):
    return jax.shard_map(
        shards,
        mesh=mesh,
        in_specs=(
            P(("dp", "tensor"), None),
            P("dp", "tensor"),
            P("dp", "tensor"),
            P("tensor", "dp"),
            P(("dp", "tensor"), None),
        ),
        out_specs=(
            P(("dp", "tensor"), None),
            P("dp", "tensor"),
            P("dp", "tensor"),
            P("tensor", "dp"),
        ),
        check_vma=False,
    )
```

```python
import jax
import jax.numpy as jnp
from jax import lax
from jax.experimental import pallas as pl
from jax.experimental.pallas import tpu as pltpu
from jax.sharding import PartitionSpec as P


def device_perm(target):
    pairs = []
    for i in range(128):
        y, h, c, z, l = i // 32, i // 16 % 2, i // 8 % 2, i // 2 % 4, i % 2
        y, h, c, z, l = target(y, h, c, z, l)
        pairs.append((i, (((y % 4 * 2 + h) * 2 + c) * 4 + z % 4) * 2 + l))
    return pairs


def send(x, target):
    return lax.ppermute(x, ("dp", "tensor"), device_perm(target))


def shift_y(x, k):
    return send(x, lambda y, h, c, z, l: (y + k, h, c, z, l))


def shift_first(x, k):
    return send(
        x, lambda y, h, c, z, l: (y, h, c, z + k, l) if c else (y + k, h, c, z, l)
    )


def shift_second(x, k):
    return send(
        x, lambda y, h, c, z, l: (y + k, h, c, z, l) if c else (y, h, c, z + k, l)
    )


def swap_h(x):
    return send(x, lambda y, h, c, z, l: (y, 1 - h, c, z, l))


def swap_c(x):
    return send(x, lambda y, h, c, z, l: (y, h, 1 - c, z, l))


def swap_l(x):
    return send(x, lambda y, h, c, z, l: (y, h, c, z, 1 - l))


def sync(*arrays):
    return lax.optimization_barrier(arrays)


def add(*terms):
    total = terms[0].astype(jnp.float32)
    for term in terms[1:]:
        total = total + term.astype(jnp.float32)
    return total.astype(jnp.bfloat16)


def exchange_y(pieces):
    groups = [[4 * i + hc for i in range(4)] for hc in range(4)]
    return lax.all_to_all(pieces, "dp", 0, 0, axis_index_groups=groups, tiled=True)


def copy_blocks(sources, moves, shapes):
    def kernel(*refs):
        ins, outs, sems = refs[: len(sources)], refs[len(sources) : -1], refs[-1]
        copies = []
        for i, (source, where, out, rows, columns) in enumerate(moves):
            copies.append(
                pltpu.make_async_copy(ins[source].at[where], outs[out].at[rows, columns], sems.at[i])
            )
        for copy in copies:
            copy.start()
        for copy in copies:
            copy.wait()

    moved = 2 * sum(2 * a * b for a, b in shapes)
    return pl.pallas_call(
        kernel,
        out_shape=[jax.ShapeDtypeStruct(shape, jnp.bfloat16) for shape in shapes],
        in_specs=[pl.BlockSpec(memory_space=pl.ANY)] * len(sources),
        out_specs=[pl.BlockSpec(memory_space=pltpu.VMEM)] * len(shapes),
        scratch_shapes=[pltpu.SemaphoreType.DMA((len(moves),))],
        compiler_params=pltpu.CompilerParams(vmem_limit_bytes=32 << 20),
        cost_estimate=pl.CostEstimate(flops=0, bytes_accessed=moved, transcendentals=0),
    )(*sources)


def shards(tokens, w_gate, w_up, w_down, cotangent):
    depth, local_ff = w_gate.shape
    rows, model = tokens.shape
    part_ff = local_ff // 4
    me = lax.axis_index("dp")
    h, c = me // 2 % 2, me % 2

    def to_relative(x):
        x = x.reshape(-1, 4, 2, 2, depth)
        x = jnp.where(h == 1, x[:, :, ::-1], x)
        x = jnp.where(c == 1, x[:, :, :, ::-1], x)
        return x.transpose(0, 3, 2, 1, 4).reshape(-1, model)

    def from_relative(x):
        x = x.reshape(-1, 2, 2, 4, depth).transpose(0, 3, 2, 1, 4)
        x = jnp.where(h == 1, x[:, :, ::-1], x)
        x = jnp.where(c == 1, x[:, :, :, ::-1], x)
        return x.reshape(-1, model)

    def columns(blocks):
        return jnp.concatenate([b[j] for b in blocks for j in range(4)], 1)

    def dot(a, b, dim_a, dim_b):
        return lax.dot_general(
            a, b, (((dim_a,), (dim_b,)), ((), ())), preferred_element_type=jnp.float32
        )

    def second_near(x):
        return shift_second(x, -1), shift_second(x, 1)

    def second_far(after, before):
        half = after.shape[0] // 2
        return shift_second(before[:half], 1), shift_second(after[half:], -1)

    half_model, quarter = model // 2, model // 4

    both_rows = to_relative(jnp.concatenate([tokens, cotangent], 0))
    gate_w = w_gate.T.reshape(4, part_ff, depth)
    up_w = w_up.T.reshape(4, part_ff, depth)
    down_w = w_down.reshape(4, part_ff, depth)
    pair_w = jnp.concatenate([gate_w, up_w], 1)
    both_l, pair_w = swap_l(both_rows), exchange_y(pair_w)

    base = jnp.concatenate(
        [both_rows[:rows], both_l[:rows], both_rows[rows:], both_l[rows:]], 0
    )
    pair_h = swap_h(pair_w)
    far, after, before, pair_w, down_w = sync(
        shift_first(base, 2), shift_first(base, -1), shift_first(base, 1), pair_w, down_w
    )

    two = 2 * rows
    tok, cot = copy_blocks(
        [base, after, far, before],
        [
            (k, pl.ds(two * i, two), i, pl.ds(two * k, two), pl.ds(0, model))
            for i in range(2)
            for k in range(4)
        ],
        [(8 * rows, model)] * 2,
    )
    tok_near, cot, pair_h, pair_w, down_w = sync(
        second_near(tok), cot, pair_h, pair_w, exchange_y(down_w)
    )

    (pair_near,) = copy_blocks(
        [pair_w, pair_h],
        [
            (i, j, 0, pl.ds(0, 2 * part_ff), pl.ds((4 * i + j) * depth, depth))
            for i in range(2)
            for j in range(4)
        ],
        [(2 * part_ff, half_model)],
    )
    pair_c = swap_c(pair_near)
    down_h = swap_h(down_w)
    cot_near = second_near(cot)
    tok_near, pair_c = sync(tok_near, pair_c)
    down_h, tok_far, cot_near, pair_c, pair_near, down_w = sync(
        down_h, second_far(*tok_near), cot_near, pair_c, pair_near, down_w
    )

    (down_near,) = copy_blocks(
        [down_w, down_h],
        [
            (i, j, 0, pl.ds(0, part_ff), pl.ds((4 * i + j) * depth, depth))
            for i in range(2)
            for j in range(4)
        ],
        [(part_ff, half_model)],
    )
    tok = jnp.concatenate([tok, tok_near[0], *tok_far, tok_near[1]], 0)
    gate_up = dot(pair_near, tok[:, :half_model], 1, 1) + dot(pair_c, tok[:, half_model:], 1, 1)
    gate = gate_up[:part_ff]
    up = gate_up[part_ff:]
    sig = jax.nn.sigmoid(gate)
    swish = gate * sig
    hidden = (swish * up).astype(jnp.bfloat16)
    slope = up * (sig + swish * (1.0 - sig))
    down_c, cot_far, hidden, swish, slope, tok = sync(
        swap_c(down_near), second_far(*cot_near), hidden, swish, slope, tok
    )

    def pieces_of(grad):
        return grad.reshape(-1, 4, depth).transpose(1, 0, 2)

    def finish(pieces):
        return pieces.reshape(-1, depth).astype(jnp.float32)

    cot = jnp.concatenate([cot, cot_near[0], *cot_far, cot_near[1]], 0)
    down_grad = dot(hidden, cot, 1, 0).astype(jnp.bfloat16)
    down_got = swap_c(down_grad[:, half_model:])
    cot_held, _ = sync(cot, down_grad)
    d_hidden = dot(down_near, cot_held[:, :half_model], 1, 1) + dot(
        down_c, cot_held[:, half_model:], 1, 1
    )
    d_up = (d_hidden * swish).astype(jnp.bfloat16)
    d_gate = (d_hidden * slope).astype(jnp.bfloat16)
    pair_d = jnp.concatenate([d_gate, d_up], 0)
    part_n = dot(pair_d, pair_near, 0, 0).astype(jnp.bfloat16)
    part_c = dot(pair_d, pair_c, 0, 0).astype(jnp.bfloat16)
    pair_d, down_got, part_n, part_c = sync(pair_d, down_got, part_n, part_c)

    down_far = swap_h(add(down_grad[:, quarter:half_model], down_got[:, quarter:]))
    pair_grad = dot(pair_d, tok, 1, 0).astype(jnp.bfloat16)

    n = part_n.shape[0] // 4
    own, after, far, before = [
        (part_n[n * k : n * (k + 1)], part_c[n * k : n * (k + 1)]) for k in range(4)
    ]
    low, high = shift_second(far[0], 1), shift_second(far[1], -1)
    pair_got = [swap_c(pair_grad[i : i + part_ff, half_model:]) for i in (0, part_ff)]
    down_far, low, high, pair_got = sync(down_far, low, high, pair_got)

    def sum_c(start):
        part = slice(start, start + part_ff)
        return (
            add(pair_grad[part, :quarter], pair_got[start // part_ff][:, :quarter]),
            add(pair_grad[part, quarter:half_model], pair_got[start // part_ff][:, quarter:]),
        )

    gate_near, gate_send = sum_c(0)
    up_near, up_send = sum_c(part_ff)
    down_grad = pieces_of(add(down_grad[:, :quarter], down_got[:, :quarter], down_far))
    after = jnp.concatenate([add(after[0], low), after[1]], 0)
    before = jnp.concatenate([before[0], add(before[1], high)], 0)
    gate_far, after, before, down_grad, up_send = sync(
        swap_h(gate_send),
        shift_second(after, 1),
        shift_second(before, -1),
        exchange_y(down_grad),
        up_send,
    )

    gate_grad = pieces_of(add(gate_near, gate_far))
    own = add(jnp.concatenate(own, 0), after, before).reshape(2, 4, -1, half_model)
    own, after, far, before = [own[:, k].reshape(-1, half_model) for k in range(4)]
    far, after, before = shift_first(far, 2), shift_first(after, 1), shift_first(before, -1)
    up_far, gate_grad, before = sync(swap_h(up_send), exchange_y(gate_grad), before)

    up_grad = exchange_y(pieces_of(add(up_near, up_far)))
    own = add(own, far, after, before).reshape(2, 2, rows, half_model)
    other = swap_l(own[:, 1].reshape(2 * rows, half_model)).reshape(2, rows, half_model)
    own = add(own[:, 0], other)
    d_tokens = from_relative(jnp.concatenate([own[0], own[1]], 1))
    d_w_down = finish(down_grad)
    d_w_gate = finish(gate_grad).T
    d_w_up = finish(up_grad).T
    return (d_tokens, d_w_gate, d_w_up, d_w_down)


def solution(mesh):
    return jax.shard_map(
        shards,
        mesh=mesh,
        in_specs=(
            P(("dp", "tensor"), None),
            P("dp", "tensor"),
            P("dp", "tensor"),
            P("tensor", "dp"),
            P(("dp", "tensor"), None),
        ),
        out_specs=(
            P(("dp", "tensor"), None),
            P("dp", "tensor"),
            P("dp", "tensor"),
            P("tensor", "dp"),
        ),
        check_vma=False,
    )
```

```python
import jax
import jax.numpy as jnp
from jax import lax
from jax.experimental import pallas as pl
from jax.experimental.pallas import tpu as pltpu
from jax.sharding import PartitionSpec as P


def device_perm(target):
    pairs = []
    for i in range(128):
        y, h, c, z, l = i // 32, i // 16 % 2, i // 8 % 2, i // 2 % 4, i % 2
        y, h, c, z, l = target(y, h, c, z, l)
        pairs.append((i, (((y % 4 * 2 + h) * 2 + c) * 4 + z % 4) * 2 + l))
    return pairs


def send(x, target):
    return lax.ppermute(x, ("dp", "tensor"), device_perm(target))


def shift_y(x, k):
    return send(x, lambda y, h, c, z, l: (y + k, h, c, z, l))


def shift_first(x, k):
    return send(
        x, lambda y, h, c, z, l: (y, h, c, z + k, l) if c else (y + k, h, c, z, l)
    )


def shift_second(x, k):
    return send(
        x, lambda y, h, c, z, l: (y + k, h, c, z, l) if c else (y, h, c, z + k, l)
    )


def swap_h(x):
    return send(x, lambda y, h, c, z, l: (y, 1 - h, c, z, l))


def swap_c(x):
    return send(x, lambda y, h, c, z, l: (y, h, 1 - c, z, l))


def swap_l(x):
    return send(x, lambda y, h, c, z, l: (y, h, c, z, 1 - l))


def sync(*arrays):
    return lax.optimization_barrier(arrays)


def add(*terms, kind=jnp.bfloat16):
    total = terms[0].astype(jnp.float32)
    for term in terms[1:]:
        total = total + term.astype(jnp.float32)
    return total.astype(kind)


def exchange_y(pieces):
    groups = [[4 * i + hc for i in range(4)] for hc in range(4)]
    return lax.all_to_all(pieces, "dp", 0, 0, axis_index_groups=groups, tiled=True)


def copy_blocks(sources, moves, shapes):
    def kernel(*refs):
        ins, outs, sems = refs[: len(sources)], refs[len(sources) : -1], refs[-1]
        copies = []
        for i, (source, where, out, rows, columns) in enumerate(moves):
            copies.append(
                pltpu.make_async_copy(ins[source].at[where], outs[out].at[rows, columns], sems.at[i])
            )
        for copy in copies:
            copy.start()
        for copy in copies:
            copy.wait()

    moved = 2 * sum(2 * a * b for a, b in shapes)
    return pl.pallas_call(
        kernel,
        out_shape=[jax.ShapeDtypeStruct(shape, jnp.bfloat16) for shape in shapes],
        in_specs=[pl.BlockSpec(memory_space=pl.ANY)] * len(sources),
        out_specs=[pl.BlockSpec(memory_space=pltpu.VMEM)] * len(shapes),
        scratch_shapes=[pltpu.SemaphoreType.DMA((len(moves),))],
        compiler_params=pltpu.CompilerParams(vmem_limit_bytes=32 << 20),
        cost_estimate=pl.CostEstimate(flops=0, bytes_accessed=moved, transcendentals=0),
    )(*sources)


def turned(pieces):
    _, n, depth = pieces.shape

    def kernel(x, out):
        for i in range(4):
            out[:, n * i : n * (i + 1)] = x[i].astype(jnp.float32).T

    return pl.pallas_call(
        kernel,
        out_shape=jax.ShapeDtypeStruct((depth, 4 * n), jnp.float32),
        in_specs=[pl.BlockSpec(memory_space=pltpu.VMEM)],
        out_specs=pl.BlockSpec(memory_space=pltpu.VMEM),
        compiler_params=pltpu.CompilerParams(vmem_limit_bytes=32 << 20),
        cost_estimate=pl.CostEstimate(
            flops=0, bytes_accessed=24 * n * depth, transcendentals=0
        ),
    )(pieces)


def shards(tokens, w_gate, w_up, w_down, cotangent):
    depth, local_ff = w_gate.shape
    rows, model = tokens.shape
    part_ff = local_ff // 4
    me = lax.axis_index("dp")
    h, c = me // 2 % 2, me % 2

    def to_relative(x):
        x = x.reshape(-1, 4, 2, 2, depth)
        x = jnp.where(h == 1, x[:, :, ::-1], x)
        x = jnp.where(c == 1, x[:, :, :, ::-1], x)
        return x.transpose(0, 3, 2, 1, 4).reshape(-1, model)

    def from_relative(x):
        x = x.reshape(-1, 2, 2, 4, depth).transpose(0, 3, 2, 1, 4)
        x = jnp.where(h == 1, x[:, :, ::-1], x)
        x = jnp.where(c == 1, x[:, :, :, ::-1], x)
        return x.reshape(-1, model)

    def columns(blocks):
        return jnp.concatenate([b[j] for b in blocks for j in range(4)], 1)

    def dot(a, b, dim_a, dim_b):
        return lax.dot_general(
            a, b, (((dim_a,), (dim_b,)), ((), ())), preferred_element_type=jnp.float32
        )

    def second_near(x):
        return shift_second(x, -1), shift_second(x, 1)

    def second_far(after, before):
        half = after.shape[0] // 2
        return shift_second(before[:half], 1), shift_second(after[half:], -1)

    half_model, quarter = model // 2, model // 4

    both_rows = jnp.concatenate([tokens, cotangent], 0)
    gate_w = w_gate.T.reshape(4, part_ff, depth)
    up_w = w_up.T.reshape(4, part_ff, depth)
    down_w = w_down.reshape(4, part_ff, depth)
    pair_w = jnp.concatenate([gate_w, up_w], 1)
    pair_w, both_rows = sync(pair_w, both_rows)
    both_l, pair_w = swap_l(both_rows), exchange_y(pair_w)

    base = to_relative(
        jnp.concatenate([both_rows[:rows], both_l[:rows], both_rows[rows:], both_l[rows:]], 0)
    )
    pair_h = swap_h(pair_w)
    far, after, before, pair_w, down_w = sync(
        shift_first(base, 2), shift_first(base, -1), shift_first(base, 1), pair_w, down_w
    )

    two = 2 * rows
    tok, cot = copy_blocks(
        [base, after, far, before],
        [
            (k, pl.ds(two * i, two), i, pl.ds(two * k, two), pl.ds(0, model))
            for i in range(2)
            for k in range(4)
        ],
        [(8 * rows, model)] * 2,
    )
    tok_near, cot, pair_h, pair_w, down_w = sync(
        second_near(tok), cot, pair_h, pair_w, exchange_y(down_w)
    )

    (pair_near,) = copy_blocks(
        [pair_w, pair_h],
        [
            (i, j, 0, pl.ds(0, 2 * part_ff), pl.ds((4 * i + j) * depth, depth))
            for i in range(2)
            for j in range(4)
        ],
        [(2 * part_ff, half_model)],
    )
    pair_c = swap_c(pair_near)
    down_h = swap_h(down_w)
    cot_near = second_near(cot)
    tok_near, pair_c = sync(tok_near, pair_c)
    tok_a = jnp.concatenate([tok, tok_near[0]], 0)

    def gate_up_of(x):
        return dot(pair_near, x[:, :half_model], 1, 1) + dot(pair_c, x[:, half_model:], 1, 1)

    gate_up_a = gate_up_of(tok_a)
    down_h, tok_far, cot_near, pair_c, pair_near, down_w, tok_a, gate_up_a = sync(
        down_h, second_far(*tok_near), cot_near, pair_c, pair_near, down_w, tok_a, gate_up_a
    )

    (down_near,) = copy_blocks(
        [down_w, down_h],
        [
            (i, j, 0, pl.ds(0, part_ff), pl.ds((4 * i + j) * depth, depth))
            for i in range(2)
            for j in range(4)
        ],
        [(part_ff, half_model)],
    )
    tok = jnp.concatenate([tok, tok_near[0], *tok_far, tok_near[1]], 0)
    gate_up = jnp.concatenate([gate_up_a, gate_up_of(tok[tok_a.shape[0] :])], 1)
    gate = gate_up[:part_ff]
    up = gate_up[part_ff:]
    sig = jax.nn.sigmoid(gate)
    swish = gate * sig
    hidden = (swish * up).astype(jnp.bfloat16)
    slope = up * (sig + swish * (1.0 - sig))
    down_c, cot_far, hidden, swish, slope, tok = sync(
        swap_c(down_near), second_far(*cot_near), hidden, swish, slope, tok
    )

    def pieces_of(grad):
        return grad.reshape(-1, 4, depth).transpose(1, 0, 2)

    def finish(pieces):
        return pieces.reshape(-1, depth).astype(jnp.float32)

    cot = jnp.concatenate([cot, cot_near[0], *cot_far, cot_near[1]], 0)
    down_grad = dot(hidden, cot, 1, 0).astype(jnp.bfloat16)
    down_got = swap_c(down_grad[:, half_model:])
    cot_held, _ = sync(cot, down_grad)
    d_hidden = dot(down_near, cot_held[:, :half_model], 1, 1) + dot(
        down_c, cot_held[:, half_model:], 1, 1
    )
    d_up = (d_hidden * swish).astype(jnp.bfloat16)
    d_gate = (d_hidden * slope).astype(jnp.bfloat16)
    pair_d = jnp.concatenate([d_gate, d_up], 0)
    middle = pair_d.shape[1] // 2

    def partial_rows(x):
        return [dot(x, w, 0, 0).astype(jnp.bfloat16) for w in (pair_near, pair_c)]

    part_b = partial_rows(pair_d[:, middle:])
    pair_d, down_got, part_b = sync(pair_d, down_got, part_b)

    down_far = swap_h(add(down_grad[:, quarter:half_model], down_got[:, quarter:]))
    pair_grad = dot(pair_d, tok, 1, 0).astype(jnp.bfloat16)

    n = middle // 2
    far, before = [tuple(part[n * k : n * (k + 1)] for part in part_b) for k in range(2)]
    low, high = shift_second(far[0], 1), shift_second(far[1], -1)
    few = part_ff // 2
    gate_got = [
        swap_c(pair_grad[i : i + few, half_model + quarter :]) for i in (0, few)
    ]
    down_far, low, high, gate_got, part_a, down_near = sync(
        down_far,
        low,
        high,
        gate_got,
        partial_rows(pair_d[:, :middle]),
        add(down_grad[:, :quarter], down_got[:, :quarter], kind=jnp.float32),
    )
    up_got = swap_c(pair_grad[part_ff:, half_model + quarter :])
    own, after = [tuple(part[n * k : n * (k + 1)] for part in part_a) for k in range(2)]
    near_got = swap_c(pair_grad[:, half_model : half_model + quarter])

    gate_send = add(pair_grad[:part_ff, quarter:half_model], jnp.concatenate(gate_got, 0))
    down_grad = pieces_of(add(down_near, down_far))
    after = jnp.concatenate([add(after[0], low), after[1]], 0)
    before = jnp.concatenate([before[0], add(before[1], high)], 0)
    gate_far, pair_sum, after, before, down_grad, up_send = sync(
        swap_h(gate_send),
        add(pair_grad[:, :quarter], near_got, kind=jnp.float32),
        shift_second(after, 1),
        shift_second(before, -1),
        exchange_y(down_grad),
        add(pair_grad[part_ff:, quarter:half_model], up_got),
    )

    gate_grad = pieces_of(add(pair_sum[:part_ff], gate_far))
    own = add(jnp.concatenate(own, 0), after, before).reshape(2, 4, -1, half_model)
    own, after, far, before = [own[:, k].reshape(-1, half_model) for k in range(4)]
    far, after, before = shift_first(far, 2), shift_first(after, 1), shift_first(before, -1)
    up_far, gate_grad, before = sync(swap_h(up_send), exchange_y(gate_grad), before)

    up_grad = exchange_y(
        pieces_of(add(pair_sum[part_ff:], up_far))
    )
    own = add(own, far, after, before).reshape(2, 2, rows, half_model)
    other = swap_l(own[:, 1].reshape(2 * rows, half_model)).reshape(2, rows, half_model)
    own = add(own[:, 0], other)
    d_tokens = from_relative(jnp.concatenate([own[0], own[1]], 1))
    d_w_down = finish(down_grad)
    d_w_gate = turned(gate_grad)
    d_w_up = turned(up_grad)
    return (d_tokens, d_w_gate, d_w_up, d_w_down)


def solution(mesh):
    return jax.shard_map(
        shards,
        mesh=mesh,
        in_specs=(
            P(("dp", "tensor"), None),
            P("dp", "tensor"),
            P("dp", "tensor"),
            P("tensor", "dp"),
            P(("dp", "tensor"), None),
        ),
        out_specs=(
            P(("dp", "tensor"), None),
            P("dp", "tensor"),
            P("dp", "tensor"),
            P("tensor", "dp"),
        ),
        check_vma=False,
    )
```

```python
import jax
import jax.numpy as jnp
from jax import lax
from jax.experimental import pallas as pl
from jax.experimental.pallas import tpu as pltpu
from jax.sharding import PartitionSpec as P


def device_perm(target):
    pairs = []
    for i in range(128):
        y, h, c, z, l = i // 32, i // 16 % 2, i // 8 % 2, i // 2 % 4, i % 2
        y, h, c, z, l = target(y, h, c, z, l)
        pairs.append((i, (((y % 4 * 2 + h) * 2 + c) * 4 + z % 4) * 2 + l))
    return pairs


def send(x, target):
    return lax.ppermute(x, ("dp", "tensor"), device_perm(target))


def shift_y(x, k):
    return send(x, lambda y, h, c, z, l: (y + k, h, c, z, l))


def shift_first(x, k):
    return send(
        x, lambda y, h, c, z, l: (y, h, c, z + k, l) if c else (y + k, h, c, z, l)
    )


def shift_second(x, k):
    return send(
        x, lambda y, h, c, z, l: (y + k, h, c, z, l) if c else (y, h, c, z + k, l)
    )


def swap_h(x):
    return send(x, lambda y, h, c, z, l: (y, 1 - h, c, z, l))


def swap_c(x):
    return send(x, lambda y, h, c, z, l: (y, h, 1 - c, z, l))


def swap_l(x):
    return send(x, lambda y, h, c, z, l: (y, h, c, z, 1 - l))


def sync(*arrays):
    return lax.optimization_barrier(arrays)


def add(*terms, kind=jnp.bfloat16):
    total = terms[0].astype(jnp.float32)
    for term in terms[1:]:
        total = total + term.astype(jnp.float32)
    return total.astype(kind)


def exchange_y(pieces):
    groups = [[4 * i + hc for i in range(4)] for hc in range(4)]
    return lax.all_to_all(pieces, "dp", 0, 0, axis_index_groups=groups, tiled=True)


def send_pieces(pieces, y):
    return [
        shift_y(lax.dynamic_index_in_dim(pieces, (y + k) % 4, 0, keepdims=True), k)
        for k in (2, 1, 3)
    ]


def place_pieces(pieces, got, y):
    for k, piece in zip((2, 1, 3), got):
        pieces = lax.dynamic_update_index_in_dim(pieces, piece, (y - k) % 4, 0)
    return pieces


def copy_blocks(sources, moves, shapes):
    def kernel(*refs):
        ins, outs, sems = refs[: len(sources)], refs[len(sources) : -1], refs[-1]
        copies = []
        for i, (source, where, out, rows, columns) in enumerate(moves):
            copies.append(
                pltpu.make_async_copy(ins[source].at[where], outs[out].at[rows, columns], sems.at[i])
            )
        for copy in copies:
            copy.start()
        for copy in copies:
            copy.wait()

    moved = 2 * sum(2 * a * b for a, b in shapes)
    return pl.pallas_call(
        kernel,
        out_shape=[jax.ShapeDtypeStruct(shape, jnp.bfloat16) for shape in shapes],
        in_specs=[pl.BlockSpec(memory_space=pl.ANY)] * len(sources),
        out_specs=[pl.BlockSpec(memory_space=pltpu.VMEM)] * len(shapes),
        scratch_shapes=[pltpu.SemaphoreType.DMA((len(moves),))],
        compiler_params=pltpu.CompilerParams(vmem_limit_bytes=32 << 20),
        cost_estimate=pl.CostEstimate(flops=0, bytes_accessed=moved, transcendentals=0),
    )(*sources)


def turned(pieces):
    _, n, depth = pieces.shape

    def kernel(x, out):
        for i in range(4):
            out[:, n * i : n * (i + 1)] = x[i].astype(jnp.float32).T

    return pl.pallas_call(
        kernel,
        out_shape=jax.ShapeDtypeStruct((depth, 4 * n), jnp.float32),
        in_specs=[pl.BlockSpec(memory_space=pltpu.VMEM)],
        out_specs=pl.BlockSpec(memory_space=pltpu.VMEM),
        compiler_params=pltpu.CompilerParams(vmem_limit_bytes=32 << 20),
        cost_estimate=pl.CostEstimate(
            flops=0, bytes_accessed=24 * n * depth, transcendentals=0
        ),
    )(pieces)


def shards(tokens, w_gate, w_up, w_down, cotangent):
    depth, local_ff = w_gate.shape
    rows, model = tokens.shape
    part_ff = local_ff // 4
    me = lax.axis_index("dp")
    y, h, c = me // 4, me // 2 % 2, me % 2

    def to_relative(x):
        x = x.reshape(-1, 4, 2, 2, depth)
        x = jnp.where(h == 1, x[:, :, ::-1], x)
        x = jnp.where(c == 1, x[:, :, :, ::-1], x)
        return x.transpose(0, 3, 2, 1, 4).reshape(-1, model)

    def from_relative(x):
        x = x.reshape(-1, 2, 2, 4, depth).transpose(0, 3, 2, 1, 4)
        x = jnp.where(h == 1, x[:, :, ::-1], x)
        x = jnp.where(c == 1, x[:, :, :, ::-1], x)
        return x.reshape(-1, model)

    def columns(blocks):
        return jnp.concatenate([b[j] for b in blocks for j in range(4)], 1)

    def dot(a, b, dim_a, dim_b):
        return lax.dot_general(
            a, b, (((dim_a,), (dim_b,)), ((), ())), preferred_element_type=jnp.float32
        )

    def second_near(x):
        return shift_second(x, -1), shift_second(x, 1)

    def second_far(after, before):
        half = after.shape[0] // 2
        return shift_second(before[:half], 1), shift_second(after[half:], -1)

    half_model, quarter = model // 2, model // 4

    both_rows = jnp.concatenate([tokens, cotangent], 0)
    gate_w = w_gate.T.reshape(4, part_ff, depth)
    up_w = w_up.T.reshape(4, part_ff, depth)
    down_w = w_down.reshape(4, part_ff, depth)
    pair_w = jnp.concatenate([gate_w, up_w], 1)
    pair_w, both_rows = sync(pair_w, both_rows)
    both_l, pair_w = swap_l(both_rows), exchange_y(pair_w)

    base = to_relative(
        jnp.concatenate([both_rows[:rows], both_l[:rows], both_rows[rows:], both_l[rows:]], 0)
    )
    pair_h = swap_h(pair_w)
    far, after, before, pair_w, down_w = sync(
        shift_first(base, 2), shift_first(base, -1), shift_first(base, 1), pair_w, down_w
    )

    two = 2 * rows
    tok, cot = copy_blocks(
        [base, after, far, before],
        [
            (k, pl.ds(two * i, two), i, pl.ds(two * k, two), pl.ds(0, model))
            for i in range(2)
            for k in range(4)
        ],
        [(8 * rows, model)] * 2,
    )
    tok_near, cot, pair_h, pair_w, down_w = sync(
        second_near(tok), cot, pair_h, pair_w, exchange_y(down_w)
    )

    (pair_near,) = copy_blocks(
        [pair_w, pair_h],
        [
            (i, j, 0, pl.ds(0, 2 * part_ff), pl.ds((4 * i + j) * depth, depth))
            for i in range(2)
            for j in range(4)
        ],
        [(2 * part_ff, half_model)],
    )
    pair_c = swap_c(pair_near)
    down_h = swap_h(down_w)
    cot_near = second_near(cot)
    tok_near, pair_c = sync(tok_near, pair_c)
    tok_a = jnp.concatenate([tok, tok_near[0]], 0)

    def gate_up_of(x):
        return dot(pair_near, x[:, :half_model], 1, 1) + dot(pair_c, x[:, half_model:], 1, 1)

    gate_up_a = gate_up_of(tok_a)
    down_h, tok_far, cot_near, pair_c, pair_near, down_w, tok_a, gate_up_a = sync(
        down_h, second_far(*tok_near), cot_near, pair_c, pair_near, down_w, tok_a, gate_up_a
    )

    (down_near,) = copy_blocks(
        [down_w, down_h],
        [
            (i, j, 0, pl.ds(0, part_ff), pl.ds((4 * i + j) * depth, depth))
            for i in range(2)
            for j in range(4)
        ],
        [(part_ff, half_model)],
    )
    tok = jnp.concatenate([tok, tok_near[0], *tok_far, tok_near[1]], 0)
    gate_up = jnp.concatenate([gate_up_a, gate_up_of(tok[tok_a.shape[0] :])], 1)
    gate = gate_up[:part_ff]
    up = gate_up[part_ff:]
    sig = jax.nn.sigmoid(gate)
    swish = gate * sig
    hidden = (swish * up).astype(jnp.bfloat16)
    slope = up * (sig + swish * (1.0 - sig))
    down_c, cot_far, hidden, swish, slope, tok = sync(
        swap_c(down_near), second_far(*cot_near), hidden, swish, slope, tok
    )

    def pieces_of(grad):
        return grad.reshape(-1, 4, depth).transpose(1, 0, 2)

    def finish(pieces):
        return pieces.reshape(-1, depth).astype(jnp.float32)

    cot = jnp.concatenate([cot, cot_near[0], *cot_far, cot_near[1]], 0)
    down_grad = dot(hidden, cot, 1, 0).astype(jnp.bfloat16)
    down_got = swap_c(down_grad[:, half_model:])
    cot_held, _ = sync(cot, down_grad)
    d_hidden = dot(down_near, cot_held[:, :half_model], 1, 1) + dot(
        down_c, cot_held[:, half_model:], 1, 1
    )
    d_up = (d_hidden * swish).astype(jnp.bfloat16)
    d_gate = (d_hidden * slope).astype(jnp.bfloat16)
    pair_d = jnp.concatenate([d_gate, d_up], 0)
    middle = pair_d.shape[1] // 2

    def partial_rows(x):
        return [dot(x, w, 0, 0).astype(jnp.bfloat16) for w in (pair_near, pair_c)]

    part_b = partial_rows(pair_d[:, middle:])
    pair_d, down_got, part_b = sync(pair_d, down_got, part_b)

    down_far = swap_h(add(down_grad[:, quarter:half_model], down_got[:, quarter:]))
    pair_grad = dot(pair_d, tok, 1, 0).astype(jnp.bfloat16)

    n = middle // 2
    far, before = [tuple(part[n * k : n * (k + 1)] for part in part_b) for k in range(2)]
    low, high = shift_second(far[0], 1), shift_second(far[1], -1)
    few = part_ff // 2
    gate_got = [
        swap_c(pair_grad[i : i + few, half_model + quarter :]) for i in (0, few)
    ]
    down_far, low, high, gate_got, part_a, down_near = sync(
        down_far,
        low,
        high,
        gate_got,
        partial_rows(pair_d[:, :middle]),
        add(down_grad[:, :quarter], down_got[:, :quarter], kind=jnp.float32),
    )
    up_got = swap_c(pair_grad[part_ff:, half_model + quarter :])
    own, after = [tuple(part[n * k : n * (k + 1)] for part in part_a) for k in range(2)]
    near_got = swap_c(pair_grad[:, half_model : half_model + quarter])

    gate_send = add(pair_grad[:part_ff, quarter:half_model], jnp.concatenate(gate_got, 0))
    down_grad = pieces_of(add(down_near, down_far))
    after = jnp.concatenate([add(after[0], low), after[1]], 0)
    before = jnp.concatenate([before[0], add(before[1], high)], 0)
    gate_far, pair_sum, after, before, down_grad, up_send = sync(
        swap_h(gate_send),
        add(pair_grad[:, :quarter], near_got, kind=jnp.float32),
        shift_second(after, 1),
        shift_second(before, -1),
        exchange_y(down_grad),
        add(pair_grad[part_ff:, quarter:half_model], up_got),
    )

    gate_grad = pieces_of(add(pair_sum[:part_ff], gate_far))
    own = add(jnp.concatenate(own, 0), after, before).reshape(2, 4, -1, half_model)
    own, after, far, before = [own[:, k].reshape(-1, half_model) for k in range(4)]
    far, after, before = shift_first(far, 2), shift_first(after, 1), shift_first(before, -1)
    up_far, gate_got, before = sync(swap_h(up_send), send_pieces(gate_grad, y), before)
    gate_grad = place_pieces(gate_grad, gate_got, y)

    up_grad = exchange_y(
        pieces_of(add(pair_sum[part_ff:], up_far))
    )
    own = add(own, far, after, before).reshape(2, 2, rows, half_model)
    other = swap_l(own[:, 1].reshape(2 * rows, half_model)).reshape(2, rows, half_model)
    own = add(own[:, 0], other)
    d_tokens = from_relative(jnp.concatenate([own[0], own[1]], 1))
    d_w_down = finish(down_grad)
    d_w_gate = turned(gate_grad)
    d_w_up = turned(up_grad)
    return (d_tokens, d_w_gate, d_w_up, d_w_down)


def solution(mesh):
    return jax.shard_map(
        shards,
        mesh=mesh,
        in_specs=(
            P(("dp", "tensor"), None),
            P("dp", "tensor"),
            P("dp", "tensor"),
            P("tensor", "dp"),
            P(("dp", "tensor"), None),
        ),
        out_specs=(
            P(("dp", "tensor"), None),
            P("dp", "tensor"),
            P("dp", "tensor"),
            P("tensor", "dp"),
        ),
        check_vma=False,
    )
```

```python
import jax
import jax.numpy as jnp
from jax import lax
from jax.experimental import pallas as pl
from jax.experimental.pallas import tpu as pltpu
from jax.sharding import PartitionSpec as P


def device_perm(target):
    pairs = []
    for i in range(128):
        y, h, c, z, l = i // 32, i // 16 % 2, i // 8 % 2, i // 2 % 4, i % 2
        y, h, c, z, l = target(y, h, c, z, l)
        pairs.append((i, (((y % 4 * 2 + h) * 2 + c) * 4 + z % 4) * 2 + l))
    return pairs


def send(x, target):
    return lax.ppermute(x, ("dp", "tensor"), device_perm(target))


def shift_y(x, k):
    return send(x, lambda y, h, c, z, l: (y + k, h, c, z, l))


def shift_first(x, k):
    return send(
        x, lambda y, h, c, z, l: (y, h, c, z + k, l) if c else (y + k, h, c, z, l)
    )


def shift_second(x, k):
    return send(
        x, lambda y, h, c, z, l: (y + k, h, c, z, l) if c else (y, h, c, z + k, l)
    )


def swap_h(x):
    return send(x, lambda y, h, c, z, l: (y, 1 - h, c, z, l))


def swap_c(x):
    return send(x, lambda y, h, c, z, l: (y, h, 1 - c, z, l))


def swap_l(x):
    return send(x, lambda y, h, c, z, l: (y, h, c, z, 1 - l))


def sync(*arrays):
    return lax.optimization_barrier(arrays)


def add(*terms, kind=jnp.bfloat16):
    total = terms[0].astype(jnp.float32)
    for term in terms[1:]:
        total = total + term.astype(jnp.float32)
    return total.astype(kind)


def exchange_y(pieces):
    groups = [[4 * i + hc for i in range(4)] for hc in range(4)]
    return lax.all_to_all(pieces, "dp", 0, 0, axis_index_groups=groups, tiled=True)


def send_pieces(pieces, y):
    return [
        shift_y(lax.dynamic_index_in_dim(pieces, (y + k) % 4, 0, keepdims=True), k)
        for k in (2, 1, 3)
    ]


def place_pieces(pieces, got, y):
    for k, piece in zip((2, 1, 3), got):
        pieces = lax.dynamic_update_index_in_dim(pieces, piece, (y - k) % 4, 0)
    return pieces


def copy_blocks(sources, moves, shapes):
    def kernel(*refs):
        ins, outs, sems = refs[: len(sources)], refs[len(sources) : -1], refs[-1]
        copies = []
        for i, (source, where, out, rows, columns) in enumerate(moves):
            copies.append(
                pltpu.make_async_copy(ins[source].at[where], outs[out].at[rows, columns], sems.at[i])
            )
        for copy in copies:
            copy.start()
        for copy in copies:
            copy.wait()

    moved = 2 * sum(2 * a * b for a, b in shapes)
    return pl.pallas_call(
        kernel,
        out_shape=[jax.ShapeDtypeStruct(shape, jnp.bfloat16) for shape in shapes],
        in_specs=[pl.BlockSpec(memory_space=pl.ANY)] * len(sources),
        out_specs=[pl.BlockSpec(memory_space=pltpu.VMEM)] * len(shapes),
        scratch_shapes=[pltpu.SemaphoreType.DMA((len(moves),))],
        compiler_params=pltpu.CompilerParams(vmem_limit_bytes=8 << 20),
        cost_estimate=pl.CostEstimate(flops=0, bytes_accessed=moved, transcendentals=0),
    )(*sources)


def turned(pieces):
    _, n, depth = pieces.shape

    def kernel(x, out):
        for i in range(4):
            out[:, n * i : n * (i + 1)] = x[i].astype(jnp.float32).T

    return pl.pallas_call(
        kernel,
        out_shape=jax.ShapeDtypeStruct((depth, 4 * n), jnp.float32),
        in_specs=[pl.BlockSpec(memory_space=pltpu.VMEM)],
        out_specs=pl.BlockSpec(memory_space=pltpu.VMEM),
        compiler_params=pltpu.CompilerParams(vmem_limit_bytes=8 << 20),
        cost_estimate=pl.CostEstimate(
            flops=0, bytes_accessed=24 * n * depth, transcendentals=0
        ),
    )(pieces)


def shards(tokens, w_gate, w_up, w_down, cotangent):
    depth, local_ff = w_gate.shape
    rows, model = tokens.shape
    part_ff = local_ff // 4
    me = lax.axis_index("dp")
    y, h, c = me // 4, me // 2 % 2, me % 2

    def to_relative(x):
        x = x.reshape(-1, 4, 2, 2, depth)
        x = jnp.where(h == 1, x[:, :, ::-1], x)
        x = jnp.where(c == 1, x[:, :, :, ::-1], x)
        return x.transpose(0, 3, 2, 1, 4).reshape(-1, model)

    def from_relative(x):
        x = x.reshape(-1, 2, 2, 4, depth).transpose(0, 3, 2, 1, 4)
        x = jnp.where(h == 1, x[:, :, ::-1], x)
        x = jnp.where(c == 1, x[:, :, :, ::-1], x)
        return x.reshape(-1, model)

    def columns(blocks):
        return jnp.concatenate([b[j] for b in blocks for j in range(4)], 1)

    def dot(a, b, dim_a, dim_b):
        return lax.dot_general(
            a, b, (((dim_a,), (dim_b,)), ((), ())), preferred_element_type=jnp.float32
        )

    def second_near(x):
        return shift_second(x, -1), shift_second(x, 1)

    def second_far(after, before):
        half = after.shape[0] // 2
        return shift_second(before[:half], 1), shift_second(after[half:], -1)

    half_model, quarter = model // 2, model // 4

    both_rows = jnp.concatenate([tokens, cotangent], 0)
    gate_w = w_gate.T.reshape(4, part_ff, depth)
    up_w = w_up.T.reshape(4, part_ff, depth)
    down_w = w_down.reshape(4, part_ff, depth)
    pair_w = jnp.concatenate([gate_w, up_w], 1)
    pair_w, both_rows = sync(pair_w, both_rows)
    both_l, pair_w = swap_l(both_rows), exchange_y(pair_w)

    base = to_relative(
        jnp.concatenate([both_rows[:rows], both_l[:rows], both_rows[rows:], both_l[rows:]], 0)
    )
    pair_h = swap_h(pair_w)
    far, after, before, pair_w, down_w = sync(
        shift_first(base, 2), shift_first(base, -1), shift_first(base, 1), pair_w, down_w
    )

    two = 2 * rows
    tok, cot = copy_blocks(
        [base, after, far, before],
        [
            (k, pl.ds(two * i, two), i, pl.ds(two * k, two), pl.ds(0, model))
            for i in range(2)
            for k in range(4)
        ],
        [(8 * rows, model)] * 2,
    )
    tok_near, cot, pair_h, pair_w, down_w = sync(
        second_near(tok), cot, pair_h, pair_w, exchange_y(down_w)
    )

    (pair_near,) = copy_blocks(
        [pair_w, pair_h],
        [
            (i, j, 0, pl.ds(0, 2 * part_ff), pl.ds((4 * i + j) * depth, depth))
            for i in range(2)
            for j in range(4)
        ],
        [(2 * part_ff, half_model)],
    )
    pair_c = swap_c(pair_near)
    down_h = swap_h(down_w)
    cot_near = second_near(cot)
    tok_near, pair_c = sync(tok_near, pair_c)
    tok_a = jnp.concatenate([tok, tok_near[0]], 0)

    def gate_up_of(x):
        return dot(pair_near, x[:, :half_model], 1, 1) + dot(pair_c, x[:, half_model:], 1, 1)

    gate_up_a = gate_up_of(tok_a)
    down_h, tok_far, cot_near, pair_c, pair_near, down_w, tok_a, gate_up_a = sync(
        down_h, second_far(*tok_near), cot_near, pair_c, pair_near, down_w, tok_a, gate_up_a
    )

    (down_near,) = copy_blocks(
        [down_w, down_h],
        [
            (i, j, 0, pl.ds(0, part_ff), pl.ds((4 * i + j) * depth, depth))
            for i in range(2)
            for j in range(4)
        ],
        [(part_ff, half_model)],
    )
    tok = jnp.concatenate([tok, tok_near[0], *tok_far, tok_near[1]], 0)
    gate_up = jnp.concatenate([gate_up_a, gate_up_of(tok[tok_a.shape[0] :])], 1)
    gate = gate_up[:part_ff]
    up = gate_up[part_ff:]
    sig = jax.nn.sigmoid(gate)
    swish = gate * sig
    hidden = (swish * up).astype(jnp.bfloat16)
    slope = up * (sig + swish * (1.0 - sig))
    down_c, cot_far, hidden, swish, slope, tok = sync(
        swap_c(down_near), second_far(*cot_near), hidden, swish, slope, tok
    )

    def pieces_of(grad):
        return grad.reshape(-1, 4, depth).transpose(1, 0, 2)

    def finish(pieces):
        return pieces.reshape(-1, depth).astype(jnp.float32)

    cot = jnp.concatenate([cot, cot_near[0], *cot_far, cot_near[1]], 0)
    down_grad = dot(hidden, cot, 1, 0).astype(jnp.bfloat16)
    down_got = swap_c(down_grad[:, half_model:])
    cot_held, _ = sync(cot, down_grad)
    d_hidden = dot(down_near, cot_held[:, :half_model], 1, 1) + dot(
        down_c, cot_held[:, half_model:], 1, 1
    )
    d_up = (d_hidden * swish).astype(jnp.bfloat16)
    d_gate = (d_hidden * slope).astype(jnp.bfloat16)
    pair_d = jnp.concatenate([d_gate, d_up], 0)
    middle = pair_d.shape[1] // 2

    def partial_rows(x):
        return [dot(x, w, 0, 0).astype(jnp.bfloat16) for w in (pair_near, pair_c)]

    part_b = partial_rows(pair_d[:, middle:])
    pair_d, down_got, part_b = sync(pair_d, down_got, part_b)

    down_far = swap_h(add(down_grad[:, quarter:half_model], down_got[:, quarter:]))
    pair_grad = dot(pair_d, tok, 1, 0).astype(jnp.bfloat16)

    n = middle // 2
    far, before = [tuple(part[n * k : n * (k + 1)] for part in part_b) for k in range(2)]
    low, high = shift_second(far[0], 1), shift_second(far[1], -1)
    few = part_ff // 2
    gate_got = [
        swap_c(pair_grad[i : i + few, half_model + quarter :]) for i in (0, few)
    ]
    down_far, low, high, gate_got, part_a, down_near = sync(
        down_far,
        low,
        high,
        gate_got,
        partial_rows(pair_d[:, :middle]),
        add(down_grad[:, :quarter], down_got[:, :quarter], kind=jnp.float32),
    )
    up_got = swap_c(pair_grad[part_ff:, half_model + quarter :])
    own, after = [tuple(part[n * k : n * (k + 1)] for part in part_a) for k in range(2)]
    near_got = swap_c(pair_grad[:, half_model : half_model + quarter])

    gate_send = add(pair_grad[:part_ff, quarter:half_model], jnp.concatenate(gate_got, 0))
    down_grad = pieces_of(add(down_near, down_far))
    after = jnp.stack([add(after[0], low), after[1]])
    before = jnp.stack([before[0], add(before[1], high)])
    gate_far, pair_sum, after, before, down_grad, up_send = sync(
        swap_h(gate_send),
        add(pair_grad[:, :quarter], near_got, kind=jnp.float32),
        shift_second(after, 1),
        shift_second(before, -1),
        exchange_y(down_grad),
        add(pair_grad[part_ff:, quarter:half_model], up_got),
    )

    gate_grad = pieces_of(add(pair_sum[:part_ff], gate_far))
    own = jnp.stack([add(own[i], after[i], before[i]) for i in range(2)])
    own = own.reshape(2, 4, -1, half_model)
    own, after, far, before = [own[:, k].reshape(-1, half_model) for k in range(4)]
    far, after, before = shift_first(far, 2), shift_first(after, 1), shift_first(before, -1)
    up_far, gate_got, before = sync(swap_h(up_send), send_pieces(gate_grad, y), before)
    gate_grad = place_pieces(gate_grad, gate_got, y)

    up_grad = exchange_y(
        pieces_of(add(pair_sum[part_ff:], up_far))
    )
    own = add(own, far, after, before).reshape(2, 2, rows, half_model)
    other = swap_l(own[:, 1].reshape(2 * rows, half_model)).reshape(2, rows, half_model)
    own = add(own[:, 0], other)
    d_tokens = from_relative(jnp.concatenate([own[0], own[1]], 1))
    d_w_down = finish(down_grad)
    d_w_gate = turned(gate_grad)
    d_w_up = turned(up_grad)
    return (d_tokens, d_w_gate, d_w_up, d_w_down)


def solution(mesh):
    return jax.shard_map(
        shards,
        mesh=mesh,
        in_specs=(
            P(("dp", "tensor"), None),
            P("dp", "tensor"),
            P("dp", "tensor"),
            P("tensor", "dp"),
            P(("dp", "tensor"), None),
        ),
        out_specs=(
            P(("dp", "tensor"), None),
            P("dp", "tensor"),
            P("dp", "tensor"),
            P("tensor", "dp"),
        ),
        check_vma=False,
    )
```

```python
import jax
import jax.numpy as jnp
from jax import lax
from jax.experimental import pallas as pl
from jax.experimental.pallas import tpu as pltpu
from jax.sharding import PartitionSpec as P


def device_perm(target):
    pairs = []
    for i in range(128):
        y, h, c, z, l = i // 32, i // 16 % 2, i // 8 % 2, i // 2 % 4, i % 2
        y, h, c, z, l = target(y, h, c, z, l)
        pairs.append((i, (((y % 4 * 2 + h) * 2 + c) * 4 + z % 4) * 2 + l))
    return pairs


def send(x, target):
    return lax.ppermute(x, ("dp", "tensor"), device_perm(target))


def shift_y(x, k):
    return send(x, lambda y, h, c, z, l: (y + k, h, c, z, l))


def shift_first(x, k):
    return send(
        x, lambda y, h, c, z, l: (y, h, c, z + k, l) if c else (y + k, h, c, z, l)
    )


def shift_second(x, k):
    return send(
        x, lambda y, h, c, z, l: (y + k, h, c, z, l) if c else (y, h, c, z + k, l)
    )


def swap_h(x):
    return send(x, lambda y, h, c, z, l: (y, 1 - h, c, z, l))


def swap_c(x):
    return send(x, lambda y, h, c, z, l: (y, h, 1 - c, z, l))


def swap_l(x):
    return send(x, lambda y, h, c, z, l: (y, h, c, z, 1 - l))


def sync(*arrays):
    return lax.optimization_barrier(arrays)


def add(*terms, kind=jnp.bfloat16):
    total = terms[0].astype(jnp.float32)
    for term in terms[1:]:
        total = total + term.astype(jnp.float32)
    return total.astype(kind)


def exchange_y(pieces):
    groups = [[4 * i + hc for i in range(4)] for hc in range(4)]
    return lax.all_to_all(pieces, "dp", 0, 0, axis_index_groups=groups, tiled=True)


def send_pieces(pieces, y):
    return [
        shift_y(lax.dynamic_index_in_dim(pieces, (y + k) % 4, 0, keepdims=True), k)
        for k in (2, 1, 3)
    ]


def place_pieces(pieces, got, y):
    for k, piece in zip((2, 1, 3), got):
        pieces = lax.dynamic_update_index_in_dim(pieces, piece, (y - k) % 4, 0)
    return pieces


def copy_blocks(sources, moves, shapes):
    def kernel(*refs):
        ins, outs, sems = refs[: len(sources)], refs[len(sources) : -1], refs[-1]
        copies = []
        for i, (source, where, out, rows, columns) in enumerate(moves):
            copies.append(
                pltpu.make_async_copy(ins[source].at[where], outs[out].at[rows, columns], sems.at[i])
            )
        for copy in copies:
            copy.start()
        for copy in copies:
            copy.wait()

    moved = 2 * sum(2 * a * b for a, b in shapes)
    return pl.pallas_call(
        kernel,
        out_shape=[jax.ShapeDtypeStruct(shape, jnp.bfloat16) for shape in shapes],
        in_specs=[pl.BlockSpec(memory_space=pl.ANY)] * len(sources),
        out_specs=[pl.BlockSpec(memory_space=pltpu.VMEM)] * len(shapes),
        scratch_shapes=[pltpu.SemaphoreType.DMA((len(moves),))],
        compiler_params=pltpu.CompilerParams(vmem_limit_bytes=8 << 20),
        cost_estimate=pl.CostEstimate(flops=0, bytes_accessed=moved, transcendentals=0),
    )(*sources)


def turned(pieces):
    _, n, depth = pieces.shape

    def kernel(x, out):
        for i in range(4):
            out[:, n * i : n * (i + 1)] = x[i].astype(jnp.float32).T

    return pl.pallas_call(
        kernel,
        out_shape=jax.ShapeDtypeStruct((depth, 4 * n), jnp.float32),
        in_specs=[pl.BlockSpec(memory_space=pltpu.VMEM)],
        out_specs=pl.BlockSpec(memory_space=pltpu.VMEM),
        compiler_params=pltpu.CompilerParams(vmem_limit_bytes=8 << 20),
        cost_estimate=pl.CostEstimate(
            flops=0, bytes_accessed=24 * n * depth, transcendentals=0
        ),
    )(pieces)


def shards(tokens, w_gate, w_up, w_down, cotangent):
    depth, local_ff = w_gate.shape
    rows, model = tokens.shape
    part_ff = local_ff // 4
    me = lax.axis_index("dp")
    y, h, c = me // 4, me // 2 % 2, me % 2

    def to_relative(x):
        x = x.reshape(-1, 4, 2, 2, depth)
        x = jnp.where(h == 1, x[:, :, ::-1], x)
        x = jnp.where(c == 1, x[:, :, :, ::-1], x)
        return x.transpose(0, 3, 2, 1, 4).reshape(-1, model)

    def from_relative(x):
        x = x.reshape(-1, 2, 2, 4, depth).transpose(0, 3, 2, 1, 4)
        x = jnp.where(h == 1, x[:, :, ::-1], x)
        x = jnp.where(c == 1, x[:, :, :, ::-1], x)
        return x.reshape(-1, model)

    def columns(blocks):
        return jnp.concatenate([b[j] for b in blocks for j in range(4)], 1)

    def dot(a, b, dim_a, dim_b):
        return lax.dot_general(
            a, b, (((dim_a,), (dim_b,)), ((), ())), preferred_element_type=jnp.float32
        )

    def second_near(x):
        return shift_second(x, -1), shift_second(x, 1)

    def second_far(after, before):
        half = after.shape[0] // 2
        return shift_second(before[:half], 1), shift_second(after[half:], -1)

    half_model, quarter = model // 2, model // 4

    both_rows = jnp.concatenate([tokens, cotangent], 0)
    gate_w = w_gate.T.reshape(4, part_ff, depth)
    up_w = w_up.T.reshape(4, part_ff, depth)
    down_w = w_down.reshape(4, part_ff, depth)
    pair_w = jnp.concatenate([gate_w, up_w], 1)
    pair_w, both_rows = sync(pair_w, both_rows)
    both_l, pair_w = swap_l(both_rows), exchange_y(pair_w)

    base = to_relative(
        jnp.concatenate([both_rows[:rows], both_l[:rows], both_rows[rows:], both_l[rows:]], 0)
    )
    pair_h = swap_h(pair_w)
    far, after, before, pair_w, down_w = sync(
        shift_first(base, 2), shift_first(base, -1), shift_first(base, 1), pair_w, down_w
    )

    two = 2 * rows
    tok, cot = copy_blocks(
        [base, after, far, before],
        [
            (k, pl.ds(two * i, two), i, pl.ds(two * k, two), pl.ds(0, model))
            for i in range(2)
            for k in range(4)
        ],
        [(8 * rows, model)] * 2,
    )
    tok_near, cot, pair_h, pair_w, down_w = sync(
        second_near(tok), cot, pair_h, pair_w, exchange_y(down_w)
    )

    (pair_near,) = copy_blocks(
        [pair_w, pair_h],
        [
            (i, j, 0, pl.ds(0, 2 * part_ff), pl.ds((4 * i + j) * depth, depth))
            for i in range(2)
            for j in range(4)
        ],
        [(2 * part_ff, half_model)],
    )
    pair_c = swap_c(pair_near)
    down_h = swap_h(down_w)
    cot_near = second_near(cot)
    tok_near, pair_c = sync(tok_near, pair_c)
    tok_a = jnp.concatenate([tok, tok_near[0]], 0)

    def gate_up_of(x):
        return dot(pair_near, x[:, :half_model], 1, 1) + dot(pair_c, x[:, half_model:], 1, 1)

    gate_up_a = gate_up_of(tok_a)
    down_h, tok_far, cot_near, pair_c, pair_near, down_w, tok_a, gate_up_a = sync(
        down_h, second_far(*tok_near), cot_near, pair_c, pair_near, down_w, tok_a, gate_up_a
    )

    (down_near,) = copy_blocks(
        [down_w, down_h],
        [
            (i, j, 0, pl.ds(0, part_ff), pl.ds((4 * i + j) * depth, depth))
            for i in range(2)
            for j in range(4)
        ],
        [(part_ff, half_model)],
    )
    tok = jnp.concatenate([tok, tok_near[0], *tok_far, tok_near[1]], 0)
    gate_up = jnp.concatenate([gate_up_a, gate_up_of(tok[tok_a.shape[0] :])], 1)
    gate = gate_up[:part_ff]
    up = gate_up[part_ff:]
    sig = jax.nn.sigmoid(gate)
    swish = gate * sig
    hidden = (swish * up).astype(jnp.bfloat16)
    slope = up * (sig + swish * (1.0 - sig))
    down_c, cot_far, hidden, swish, slope, tok = sync(
        swap_c(down_near), second_far(*cot_near), hidden, swish, slope, tok
    )

    def pieces_of(grad):
        return grad.reshape(-1, 4, depth).transpose(1, 0, 2)

    def finish(pieces):
        return pieces.reshape(-1, depth).astype(jnp.float32)

    cot = jnp.concatenate([cot, cot_near[0], *cot_far, cot_near[1]], 0)
    down_grad = dot(hidden, cot, 1, 0).astype(jnp.bfloat16)
    down_got = swap_c(down_grad[:, half_model:])
    cot_held, _ = sync(cot, down_grad)
    d_hidden = dot(down_near, cot_held[:, :half_model], 1, 1) + dot(
        down_c, cot_held[:, half_model:], 1, 1
    )
    d_up = (d_hidden * swish).astype(jnp.bfloat16)
    d_gate = (d_hidden * slope).astype(jnp.bfloat16)
    pair_d = jnp.concatenate([d_gate, d_up], 0)
    middle = pair_d.shape[1] // 2

    def partial_rows(x):
        return [dot(x, w, 0, 0).astype(jnp.bfloat16) for w in (pair_near, pair_c)]

    part_b = partial_rows(pair_d[:, middle:])
    pair_d, down_got, part_b = sync(pair_d, down_got, part_b)

    down_far = swap_h(add(down_grad[:, quarter:half_model], down_got[:, quarter:]))
    pair_grad = dot(pair_d, tok, 1, 0).astype(jnp.bfloat16)

    n = middle // 2
    far, before = [tuple(part[n * k : n * (k + 1)] for part in part_b) for k in range(2)]
    low, high = shift_second(far[0], 1), shift_second(far[1], -1)
    few = part_ff // 2
    gate_got = [
        swap_c(pair_grad[i : i + few, half_model + quarter :]) for i in (0, few)
    ]
    down_far, low, high, gate_got, part_a, down_near = sync(
        down_far,
        low,
        high,
        gate_got,
        partial_rows(pair_d[:, :middle]),
        add(down_grad[:, :quarter], down_got[:, :quarter], kind=jnp.float32),
    )
    up_got = swap_c(pair_grad[part_ff:, half_model + quarter :])
    own, after = [tuple(part[n * k : n * (k + 1)] for part in part_a) for k in range(2)]
    near_got = swap_c(pair_grad[:, half_model : half_model + quarter])

    gate_send = add(pair_grad[:part_ff, quarter:half_model], jnp.concatenate(gate_got, 0))
    down_grad = pieces_of(add(down_near, down_far))
    after = jnp.stack([add(after[0], low), after[1]])
    before = jnp.stack([before[0], add(before[1], high)])
    gate_far, pair_sum, after, before, down_grad, up_send = sync(
        swap_h(gate_send),
        add(pair_grad[:, :quarter], near_got, kind=jnp.float32),
        shift_second(after, 1),
        shift_second(before, -1),
        exchange_y(down_grad),
        add(pair_grad[part_ff:, quarter:half_model], up_got),
    )

    gate_grad = pieces_of(add(pair_sum[:part_ff], gate_far))
    own = jnp.stack([add(own[i], after[i], before[i]) for i in range(2)])
    own = own.reshape(2, 4, -1, half_model)
    own, after, far, before = [own[:, k].reshape(-1, half_model) for k in range(4)]
    far, after, before = shift_first(far, 2), shift_first(after, 1), shift_first(before, -1)
    up_far, gate_got, far = sync(swap_h(up_send), send_pieces(gate_grad, y), far)
    gate_grad = place_pieces(gate_grad, gate_got, y)

    up_grad = exchange_y(
        pieces_of(add(pair_sum[part_ff:], up_far))
    )
    own = add(own, far, after, before).reshape(2, 2, rows, half_model)
    other = swap_l(own[:, 1].reshape(2 * rows, half_model)).reshape(2, rows, half_model)
    own = add(own[:, 0], other)
    d_tokens = from_relative(jnp.concatenate([own[0], own[1]], 1))
    d_w_down = finish(down_grad)
    d_w_gate = turned(gate_grad)
    d_w_up = turned(up_grad)
    return (d_tokens, d_w_gate, d_w_up, d_w_down)


def solution(mesh):
    return jax.shard_map(
        shards,
        mesh=mesh,
        in_specs=(
            P(("dp", "tensor"), None),
            P("dp", "tensor"),
            P("dp", "tensor"),
            P("tensor", "dp"),
            P(("dp", "tensor"), None),
        ),
        out_specs=(
            P(("dp", "tensor"), None),
            P("dp", "tensor"),
            P("dp", "tensor"),
            P("tensor", "dp"),
        ),
        check_vma=False,
    )
```
